256 devices in a mesh: fsdp: 32 (over z, x_hi, core), tp: 8 (over y, x_lo).
Axes of the slice: x: 4 (x_hi: 2, x_lo: 2; x = x_hi * 2 + x_lo), y: 4, z: 8, core: 2. Of those that a mesh axis runs over, the one named last changes fastest.
Arguments:
- activations: bfloat16 [32768, 4096], P('fsdp', 'tp'), may hold values from -6 to 6
- cotangent: bfloat16 [32768, 8192], P('fsdp', 'tp'), may hold values from -0.03125 to 0.03125
- weight: bfloat16 [4096, 8192], P('fsdp', 'tp'), may hold values from -0.09375 to 0.09375
- queries: bfloat16 [512, 4, 8, 4, 128], P('fsdp', None, 'tp'), may hold values from -200 to 200
- new_keys: bfloat16 [512, 4, 8, 128], P('fsdp', None, 'tp'), may hold values from -6 to 6
- new_values: bfloat16 [512, 4, 8, 128], P('fsdp', None, 'tp'), may hold values from -24 to 24
- key_cache: bfloat16 [512, 8, 512, 128], P('fsdp', 'tp'), may hold values from -6 to 6
- value_cache: bfloat16 [512, 8, 512, 128], P('fsdp', 'tp'), may hold values from -24 to 24
- cache_lengths: int32 [512], P('fsdp'), may hold values from 2 to 512, as said below
Outputs:
- grad_weight: float32 [4096, 8192], P('fsdp', 'tp')
- decoded: bfloat16 [512, 4, 8192], P('fsdp', None, 'tp')
The draws below stay inside these ranges and needn't reach their ends.
Inputs may be any that keep to these rules, and one draw needn't show every extreme that they name: `cache_lengths`: some row holds exactly 512 cached positions and some row exactly 2.
All inputs are finite; a program needn't handle non-finite values.
Results may differ from the reference program's by a relative error of at most 0.025.
Values may be sent and summed in bfloat16 or wider, within the bound.
No kernel may reach another device: no remote copies, remote signals or barrier semaphores. Data moves between devices by JAX's collectives and lax.ppermute only.
A program may use at most 128 MiB of HBM per device.

```python
import jax
import jax.numpy as jnp
from jax import lax

D = 8192
KVH = 8
HD = 128
QPK = 4
QB = 128
STEPS = 4
TOK_DEV = 1024
CACHE = 512
DIN = 4096
TOKENS = 32768
ROWS = 512
N_FSDP = 32


def cache_normal(key):
    return jnp.clip(jax.random.normal(key, (ROWS, KVH, CACHE, HD), jnp.float32), -6.0, 6.0)


def draw_key_cache(key, part):
    shared = cache_normal(key)
    return shared.astype(jnp.bfloat16)


def draw_queries(key, part):
    key = jax.random.fold_in(key, 2)
    shape = (ROWS, STEPS, KVH, QPK, HD)
    base = jnp.clip(jax.random.normal(key, shape, jnp.float32), -6.0, 6.0) * 1.5
    return base.astype(jnp.bfloat16)


def draw_cache_lengths(key, part):
    key = jax.random.fold_in(key, 3)
    first_key, second_key = jax.random.split(key)
    lengths = jax.random.randint(first_key, (ROWS,), 2, CACHE + 1, jnp.int32)
    picked = jax.random.permutation(second_key, ROWS)
    lengths = lengths.at[picked[0]].set(CACHE)
    lengths = lengths.at[picked[1]].set(2)
    return lengths


def block_levels(rng, shape, pieces, low, high):
    def one(position, blocks):
        heights = jax.random.uniform(jax.random.fold_in(jax.random.fold_in(rng, 6), position), (blocks,), jnp.float32, low / len(pieces), high / len(pieces))
        return jnp.repeat(jnp.exp(heights), shape[position] // blocks).reshape((-1,) + (1,) * (len(shape) - position - 1))

    factor_of = one(*pieces[0])
    for cut in pieces[1:]:
        factor_of = factor_of * one(*cut)
    return factor_of


def bell_draw(own_key, extent, scale, most, shards=(), kind=jnp.bfloat16):
    factor_of = block_levels(own_key, extent, shards, -0.22, 0.18) if shards else 1.0
    result = jax.random.normal(own_key, extent, jnp.float32) * scale * factor_of
    return jnp.minimum(jnp.maximum(result, -most), most).astype(kind)


def setup_inputs(seed: int = 0) -> dict:
    arg_keys = jax.random.split(jax.random.key(seed), 10)
    activations = bell_draw(arg_keys[0], (TOKENS, DIN), 1.0, 6.0, ((0, 32), (1, 8)))
    cotangent = bell_draw(arg_keys[1], (TOKENS, D), TOKENS ** -0.5, 0.03125, ((0, 32), (1, 8)))
    weight = bell_draw(arg_keys[2], (DIN, D), DIN ** -0.5, 0.09375, ((0, 32), (1, 8)))
    queries = draw_queries(jax.random.fold_in(arg_keys[9], 71), 0)
    new_keys = bell_draw(arg_keys[4], (ROWS, STEPS, KVH, HD), 1.0, 6.0, ((0, 32), (2, 8)))
    new_values = bell_draw(arg_keys[5], (ROWS, STEPS, KVH, HD), 4.0, 24.0, ((0, 32), (2, 8)))
    key_cache = draw_key_cache(jax.random.fold_in(arg_keys[9], 71), 0)
    value_cache = bell_draw(arg_keys[7], (ROWS, KVH, CACHE, HD), 4.0, 24.0, ((0, 32), (1, 8)))
    cache_lengths = draw_cache_lengths(jax.random.fold_in(arg_keys[9], 71), 0)
    return {"activations": activations, "cotangent": cotangent, "weight": weight, "queries": queries, "new_keys": new_keys, "new_values": new_values, "key_cache": key_cache, "value_cache": value_cache, "cache_lengths": cache_lengths}


learn_rate = 0.01
scale_limit = 448.0
epsilon = 1e-6


def block_quantize(updated):
    height, breadth = updated.shape
    blocks = updated.reshape(height // QB, QB, breadth // QB, QB)
    largest = jnp.max(jnp.abs(blocks), axis=(1, 3))
    scales = ((largest + epsilon) / scale_limit).astype(jnp.bfloat16)
    quantized = (blocks / scales.astype(jnp.float32)[:, None, :, None]).astype(jnp.bfloat16)
    return quantized.reshape(height, breadth), scales


def attend(queries, new_keys, new_values, key_cache, value_cache, cache_lengths):
    factor = HD ** -0.5
    query_f = queries.astype(jnp.float32)
    scores_cache = jnp.einsum('rsgqd,rgpd->rsgqp', query_f, key_cache.astype(jnp.float32)) * factor
    scores_new = jnp.einsum('rsgqd,rjgd->rsgqj', query_f, new_keys.astype(jnp.float32)) * factor
    places = jnp.arange(key_cache.shape[2], dtype=jnp.int32)
    valid = places[None, :] < cache_lengths[:, None]
    scores_cache = jnp.where(valid[:, None, None, None, :], scores_cache, -jnp.inf)
    count = queries.shape[1]
    order = jnp.arange(count, dtype=jnp.int32)
    causal = order[None, :] <= order[:, None]
    scores_new = jnp.where(causal[None, :, None, None, :], scores_new, -jnp.inf)
    top = jnp.maximum(jnp.max(scores_cache, axis=-1), jnp.max(scores_new, axis=-1))
    exp_cache = jnp.exp(scores_cache - top[..., None])
    exp_new = jnp.exp(scores_new - top[..., None])
    total = jnp.sum(exp_cache, axis=-1) + jnp.sum(exp_new, axis=-1)
    probs_cache = (exp_cache / total[..., None]).astype(jnp.bfloat16)
    probs_new = (exp_new / total[..., None]).astype(jnp.bfloat16)
    mixed = jnp.einsum('rsgqp,rgpd->rsgqd', probs_cache.astype(jnp.float32), value_cache.astype(jnp.float32))
    mixed = mixed + jnp.einsum('rsgqj,rjgd->rsgqd', probs_new.astype(jnp.float32), new_values.astype(jnp.float32))
    return mixed.astype(jnp.bfloat16)


def reference(activations, cotangent, weight, queries, new_keys, new_values, key_cache, value_cache, cache_lengths):
    act_blocks = activations.reshape(N_FSDP, TOK_DEV, DIN)
    cot_blocks = cotangent.reshape(N_FSDP, TOK_DEV, D)

    def add_block(total, pair):
        act_block, cot_block = pair
        part = jnp.dot(act_block.T, cot_block, preferred_element_type=jnp.float32).astype(jnp.bfloat16)
        return total + lax.optimization_barrier(part).astype(jnp.float32), None

    grad_weight, unused = lax.scan(add_block, jnp.zeros((DIN, D), jnp.float32), (act_blocks, cot_blocks))
    updated = weight.astype(jnp.float32) - learn_rate * grad_weight
    quantized, scales = block_quantize(updated)
    attended = attend(queries, new_keys, new_values, key_cache, value_cache, cache_lengths)
    count = ROWS * STEPS
    flat = attended.reshape(count, DIN)
    row_blocks = DIN // QB
    col_blocks = D // QB
    left = flat.reshape(count, row_blocks, QB).transpose(1, 0, 2)
    right = quantized.reshape(row_blocks, QB, D)

    def add_rows(total, trio):
        left_block, right_block, scale_block = trio
        product = jnp.dot(left_block, right_block, preferred_element_type=jnp.float32)
        scaled = product.reshape(count, col_blocks, QB) * scale_block.astype(jnp.float32)[None, :, None]
        return total + scaled.reshape(count, D), None

    summed, unused = lax.scan(add_rows, jnp.zeros((count, D), jnp.float32), (left, right, scales))
    decoded = summed.astype(jnp.bfloat16).reshape(ROWS, STEPS, D)
    return (grad_weight, decoded)
```

```python
import jax
import jax.numpy as jnp
from jax import lax
from jax.sharding import Mesh, PartitionSpec as P

QB = 128
NZ = 8
NY = 4

learn_rate = 0.01
scale_limit = 448.0
epsilon = 1e-06

F32 = jnp.float32
BF16 = jnp.bfloat16


def shift(x, axis, size, step):
    return lax.ppermute(x, axis, [(i, (i + step) % size) for i in range(size)])


def swap(x, axis):
    return lax.ppermute(x, axis, [(0, 1), (1, 0)])


def pick(x, index, axis=0):
    return lax.dynamic_index_in_dim(x, index, axis, keepdims=False)


def attend(queries, new_keys, new_values, key_cache, value_cache, cache_lengths):
    factor = queries.shape[-1] ** (-0.5)
    scores_cache = (
        jnp.einsum("rsgqd,rgpd->rsgqp", queries, key_cache, preferred_element_type=F32)
        * factor
    )
    scores_new = (
        jnp.einsum("rsgqd,rjgd->rsgqj", queries, new_keys, preferred_element_type=F32)
        * factor
    )
    places = jnp.arange(key_cache.shape[2], dtype=jnp.int32)
    valid = places[None, :] < cache_lengths[:, None]
    scores_cache = jnp.where(valid[:, None, None, None, :], scores_cache, -jnp.inf)
    count = queries.shape[1]
    order = jnp.arange(count, dtype=jnp.int32)
    causal = order[None, :] <= order[:, None]
    scores_new = jnp.where(causal[None, :, None, None, :], scores_new, -jnp.inf)
    top = jnp.maximum(jnp.max(scores_cache, axis=-1), jnp.max(scores_new, axis=-1))
    exp_cache = jnp.exp(scores_cache - top[..., None])
    exp_new = jnp.exp(scores_new - top[..., None])
    total = jnp.sum(exp_cache, axis=-1) + jnp.sum(exp_new, axis=-1)
    probs_cache = (exp_cache / total[..., None]).astype(BF16)
    probs_new = (exp_new / total[..., None]).astype(BF16)
    mixed = jnp.einsum(
        "rsgqp,rgpd->rsgqd", probs_cache, value_cache, preferred_element_type=F32
    )
    mixed = mixed + jnp.einsum(
        "rsgqj,rjgd->rsgqd", probs_new, new_values, preferred_element_type=F32
    )
    return mixed.astype(BF16)


def gather_y(x):
    half = x.shape[0] // 2
    down = shift(x, "y", NY, 1)
    up = shift(x, "y", NY, -1)
    far_a = shift(down[:half], "y", NY, 1)
    far_b = shift(up[half:], "y", NY, -1)
    return x, down, jnp.concatenate([far_a, far_b], axis=0), up


def scatter_z(x, z):
    half = x.shape[1] // 2

    def block(k):
        return pick(x, (z + k) % NZ).astype(F32)

    far = pick(x, (z + 4) % NZ)
    fwd = shift(far[:half], "z", NZ, 1).astype(F32)
    bwd = shift(far[half:], "z", NZ, -1).astype(F32)
    mine = block(3)
    fwd = jnp.concatenate([mine[:half] + fwd, mine[half:]], axis=0)
    mine = block(-3)
    bwd = jnp.concatenate([mine[:half], mine[half:] + bwd], axis=0)
    for k in (2, 1):
        fwd = block(k) + shift(fwd.astype(BF16), "z", NZ, 1).astype(F32)
        bwd = block(-k) + shift(bwd.astype(BF16), "z", NZ, -1).astype(F32)
    fwd = shift(fwd.astype(BF16), "z", NZ, 1).astype(F32)
    bwd = shift(bwd.astype(BF16), "z", NZ, -1).astype(F32)
    return block(0) + fwd + bwd


def per_device(
    activations,
    cotangent,
    weight,
    queries,
    new_keys,
    new_values,
    key_cache,
    value_cache,
    cache_lengths,
):
    z, xh, core, y, xl = (lax.axis_index(a) for a in ("z", "xh", "c", "y", "xl"))
    cot_other = swap(cotangent, "xl")
    acts = gather_y(activations)

    blocks = weight.reshape(QB, NZ, QB).transpose(1, 0, 2)
    blocks = lax.all_to_all(blocks, "z", 0, 0, tiled=True)
    blocks = blocks.reshape(NY, 2, QB, QB)
    kept, sent = pick(blocks, xl, 1), pick(blocks, 1 - xl, 1)
    blocks = jnp.stack([kept, swap(sent, "xl")], axis=1)
    weight_here = jnp.stack([pick(blocks, (y - k) % NY) for k in range(NY)], axis=0)

    attended = attend(queries, new_keys, new_values, key_cache, value_cache, cache_lengths)
    local_rows, local_steps = queries.shape[0], queries.shape[1]
    count = local_rows * local_steps
    heads = attended.reshape(count, 2, 2, QB)
    heads = jnp.concatenate([pick(heads, core, 2), pick(heads, 1 - core, 2)], axis=-1)
    kept, sent = pick(heads, xh, 1), pick(heads, 1 - xh, 1)
    got = swap(sent, "xh")
    mixed = jnp.stack([kept, got], axis=0)
    mixed = lax.all_gather(mixed, "z", axis=0, tiled=False)
    mixed = mixed.transpose(1, 0, 2, 3).reshape(2 * NZ * count, 2 * QB)
    lefts = gather_y(mixed)

    sums = []
    for cot in (cotangent, cot_other):
        parts = []
        for act in acts:
            part = lax.dot_general(
                act, cot, (((0,), (0,)), ((), ())), preferred_element_type=F32
            ).astype(BF16)
            parts.append(part.reshape(2, 2, QB, NZ, QB).transpose(1, 3, 0, 2, 4))
        part = jnp.stack(parts, axis=2).reshape(2, NZ, NY * 2 * QB, QB)
        kept, sent = pick(part, core), pick(part, 1 - core)
        part = (kept.astype(F32) + swap(sent, "c").astype(F32)).astype(BF16)
        part = scatter_z(part, z).reshape(NY, 2, QB, QB)
        kept, sent = pick(part, xh, 1), pick(part, 1 - xh, 1)
        sums.append(kept + swap(sent.astype(BF16), "xh").astype(F32))
    grad = jnp.stack(sums, axis=1)

    blocks = grad.astype(BF16)
    blocks = jnp.stack([pick(blocks, (y - k) % NY) for k in range(NY)], axis=0)
    kept, got = blocks[:, 0], swap(blocks[:, 1], "xl")
    first = jnp.where(xl == 0, kept, got)
    second = jnp.where(xl == 0, got, kept)
    blocks = jnp.stack([first, second], axis=1).reshape(NZ, QB, QB)
    blocks = lax.all_to_all(blocks, "z", 0, 0, tiled=True)
    grad_weight = blocks.transpose(1, 0, 2).reshape(QB, NZ * QB).astype(F32)

    updated = weight_here.astype(F32) - learn_rate * grad
    largest = jnp.max(jnp.abs(updated), axis=(2, 3))
    scales = ((largest + epsilon) / scale_limit).astype(BF16)
    quantized = (updated / scales.astype(F32)[:, :, None, None]).astype(BF16)
    quantized_other, scales_other = swap(quantized, "c"), swap(scales, "c")

    total = 0.0
    for k in range(NY):
        for j, (quant, scale) in enumerate(((quantized, scales), (quantized_other, scales_other))):
            left = lefts[k][:, j * QB : (j + 1) * QB]
            right = quant[k].transpose(1, 0, 2).reshape(QB, 2 * QB)
            product = jnp.dot(left, right, preferred_element_type=F32)
            total = total + product * jnp.repeat(scale[k].astype(F32), QB)[None, :]
    total = total.reshape(2, NZ * count, 2, QB).transpose(0, 2, 1, 3)
    sent = total.astype(BF16)
    summed = (
        total[0, 0]
        + swap(sent[0, 1], "xl").astype(F32)
        + swap(sent[1, 0], "xh").astype(F32)
        + lax.ppermute(
            sent[1, 1], ("xh", "xl"), [(i, 3 - i) for i in range(4)]
        ).astype(F32)
    )
    out = summed.astype(BF16).reshape(NZ, count, QB)
    out = lax.all_to_all(out, "z", 0, 0, tiled=True)
    decoded = out.transpose(1, 0, 2).reshape(local_rows, local_steps, NZ * QB)
    return (grad_weight, decoded)


def solution(mesh):
    inner = Mesh(mesh.devices.reshape(8, 2, 2, 4, 2), ("z", "xh", "c", "y", "xl"))
    fsdp, tp = ("z", "xh", "c"), ("y", "xl")
    return jax.shard_map(
        per_device,
        mesh=inner,
        in_specs=(
            P(fsdp, tp),
            P(fsdp, tp),
            P(fsdp, tp),
            P(fsdp, None, tp, None, None),
            P(fsdp, None, tp, None),
            P(fsdp, None, tp, None),
            P(fsdp, tp, None, None),
            P(fsdp, tp, None, None),
            P(fsdp),
        ),
        out_specs=(P(fsdp, tp), P(fsdp, None, tp)),
        check_vma=False,
    )
```

```python
import functools

import jax
import jax.numpy as jnp
from jax import lax
from jax.experimental import pallas as pl
from jax.experimental.pallas import tpu as pltpu
from jax.sharding import Mesh, PartitionSpec as P

QB = 128
NZ = 8
NY = 4

learn_rate = 0.01
scale_limit = 448.0
epsilon = 1e-06

F32 = jnp.float32
BF16 = jnp.bfloat16
NT = (((1,), (1,)), ((), ()))


def shift(x, axis, size, step):
    return lax.ppermute(x, axis, [(i, (i + step) % size) for i in range(size)])


def swap(x, axis):
    return lax.ppermute(x, axis, [(0, 1), (1, 0)])


def pick(x, index, axis=0):
    return lax.dynamic_index_in_dim(x, index, axis, keepdims=False)


def attend_kernel(steps, len_ref, q_ref, nk_ref, nv_ref, k_ref, v_ref, out_ref):
    rows, count, head = q_ref.shape
    factor = head ** (-0.5)
    first = pl.program_id(0) * rows
    places = lax.broadcasted_iota(jnp.int32, (count, k_ref.shape[1]), 1)
    step = lax.broadcasted_iota(jnp.int32, (count, nk_ref.shape[1]), 0) % steps
    later = lax.broadcasted_iota(jnp.int32, (count, nk_ref.shape[1]), 1) > step
    for r in range(rows):
        q = q_ref[r]
        old = lax.dot_general(q, k_ref[r], NT, preferred_element_type=F32) * factor
        new = lax.dot_general(q, nk_ref[r], NT, preferred_element_type=F32) * factor
        old = jnp.where(places < len_ref[first + r], old, -jnp.inf)
        new = jnp.where(later, -jnp.inf, new)
        top = jnp.maximum(
            jnp.max(old, axis=1, keepdims=True), jnp.max(new, axis=1, keepdims=True)
        )
        old, new = jnp.exp(old - top), jnp.exp(new - top)
        total = jnp.sum(old, axis=1, keepdims=True) + jnp.sum(new, axis=1, keepdims=True)
        old, new = (old / total).astype(BF16), (new / total).astype(BF16)
        mixed = jnp.dot(old, v_ref[r], preferred_element_type=F32)
        mixed = mixed + jnp.dot(new, nv_ref[r], preferred_element_type=F32)
        out_ref[r] = mixed.astype(BF16)


def attend(queries, new_keys, new_values, key_cache, value_cache, cache_lengths):
    rows, steps, _, heads, size = queries.shape
    cache = key_cache.shape[2]
    tile = 4
    q = queries[:, :, 0].transpose(0, 2, 1, 3).reshape(rows, heads * steps, size)
    pad = ((0, 0), (0, 16 - steps), (0, 0))
    nk, nv = jnp.pad(new_keys[:, :, 0], pad), jnp.pad(new_values[:, :, 0], pad)

    def block(height):
        return pl.BlockSpec((tile, height, size), lambda i: (i, 0, 0))

    return pl.pallas_call(
        functools.partial(attend_kernel, steps),
        grid=(rows // tile,),
        out_shape=jax.ShapeDtypeStruct((rows, heads * steps, size), BF16),
        in_specs=[pl.BlockSpec(memory_space=pltpu.SMEM)]
        + [block(heads * steps), block(16), block(16), block(cache), block(cache)],
        out_specs=block(heads * steps),
        cost_estimate=pl.CostEstimate(
            flops=4 * rows * heads * steps * cache * size,
            bytes_accessed=4 * rows * cache * size,
            transcendentals=rows * heads * steps * cache,
        ),
    )(cache_lengths, q, nk, nv, key_cache[:, 0], value_cache[:, 0])


def grad_kernel(names, core_ref, *refs):
    lefts = sorted({left for left, _ in names})
    rights = sorted({right for _, right in names})
    left_refs = dict(zip(lefts, refs))
    right_refs = dict(zip(rights, refs[len(lefts) :]))
    keep_ref, send_ref = refs[-2:]
    own = core_ref[0] == 0
    columns = keep_ref.shape[0]
    for n, (left, right) in enumerate(names):
        part = jnp.dot(
            left_refs[left][...], right_refs[right][...], preferred_element_type=F32
        ).astype(BF16)
        for v in range(columns):
            for w in range(2):
                first = part[2 * w * QB : (2 * w + 1) * QB, v * QB : (v + 1) * QB]
                second = part[(2 * w + 1) * QB : (2 * w + 2) * QB, v * QB : (v + 1) * QB]
                rows = slice((2 * n + w) * QB, (2 * n + w + 1) * QB)
                keep_ref[v, rows] = jnp.where(own, first, second)
                send_ref[v, rows] = jnp.where(own, second, first)


def grad_parts(core, names, lefts, rights):
    left_names = sorted({left for left, _ in names})
    right_names = sorted({right for _, right in names})
    height, depth = lefts[0].shape
    breadth = rights[0].shape[1]
    tile = 2 * QB
    shape = jax.ShapeDtypeStruct((breadth // QB, len(names) * height // 2, QB), BF16)
    out = pl.BlockSpec((tile // QB, shape.shape[1], QB), lambda i: (i, 0, 0))
    return pl.pallas_call(
        functools.partial(grad_kernel, names),
        grid=(breadth // tile,),
        out_shape=(shape, shape),
        in_specs=[pl.BlockSpec(memory_space=pltpu.SMEM)]
        + [pl.BlockSpec((height, depth), lambda i: (0, 0))] * len(left_names)
        + [pl.BlockSpec((depth, tile), lambda i: (0, i))] * len(right_names),
        out_specs=(out, out),
        compiler_params=pltpu.CompilerParams(vmem_limit_bytes=40 * 2**20),
        cost_estimate=pl.CostEstimate(
            flops=2 * len(names) * height * depth * breadth,
            bytes_accessed=2 * (len(left_names) * height * depth + len(names) * height * breadth),
            transcendentals=0,
        ),
    )(
        core.reshape(1),
        *[lefts[n] for n in left_names],
        *[rights[n] for n in right_names],
    )


def project_kernel(own_ref, scale_ref, *refs):
    left_refs, (quant_ref, quant_other_ref, out_ref) = refs[:NY], refs[NY:]
    rows = left_refs[0].shape[0]
    total = jnp.zeros((rows, 2 * QB), F32)
    for k in range(NY):
        for j, quant in enumerate((quant_ref, quant_other_ref)):
            right = jnp.concatenate([quant[k, 0], quant[k, 1]], axis=1)
            product = jnp.dot(
                left_refs[k][:, j * QB : (j + 1) * QB], right, preferred_element_type=F32
            )
            total = total + product * scale_ref[2 * k + j : 2 * k + j + 1, :]
    total = total.astype(BF16)
    swapped = own_ref[0] == 1
    first, second = total[:, :QB], total[:, QB:]
    low, high = jnp.where(swapped, second, first), jnp.where(swapped, first, second)
    count = out_ref.shape[3]
    for v in range(out_ref.shape[0]):
        for w in range(2):
            at = (2 * v + w) * count
            out_ref[v, w, 0] = low[at : at + count]
            out_ref[v, w, 1] = high[at : at + count]


def project(xl, lefts, quantized, quantized_other, scales, count):
    tile = 2
    whole = pl.BlockSpec(quantized.shape, lambda i: (0, 0, 0, 0))
    return pl.pallas_call(
        project_kernel,
        grid=(NZ // tile,),
        out_shape=jax.ShapeDtypeStruct((NZ, 2, 2, count, QB), BF16),
        in_specs=[
            pl.BlockSpec(memory_space=pltpu.SMEM),
            pl.BlockSpec(scales.shape, lambda i: (0, 0)),
        ]
        + [pl.BlockSpec((tile * 2 * count, 2 * QB), lambda i: (i, 0))] * NY
        + [whole, whole],
        out_specs=pl.BlockSpec((tile, 2, 2, count, QB), lambda i: (i, 0, 0, 0, 0)),
        cost_estimate=pl.CostEstimate(
            flops=2 * NZ * 2 * count * 2 * QB * 8 * QB,
            bytes_accessed=4 * 2**20,
            transcendentals=0,
        ),
    )(xl.reshape(1), scales, *lefts, quantized, quantized_other)


def gather_z(x, z):
    half = x.shape[0] // 2
    down, up = [x], [x]
    for k in range(3):
        down.append(shift(down[-1], "z", NZ, 1))
        up.append(shift(up[-1], "z", NZ, -1))
    far = jnp.concatenate(
        [shift(down[3][:half], "z", NZ, 1), shift(up[3][half:], "z", NZ, -1)], axis=0
    )
    ring = [x, up[1], up[2], up[3], far, down[3], down[2], down[1]]
    ring = jnp.stack(ring + ring, axis=0)
    return lax.dynamic_slice_in_dim(ring, NZ - z, NZ, axis=0)


def gather_y(x):
    half = x.shape[0] // 2
    down = shift(x, "y", NY, 1)
    up = shift(x, "y", NY, -1)
    far_a = shift(down[:half], "y", NY, 1)
    far_b = shift(up[half:], "y", NY, -1)
    return x, down, jnp.concatenate([far_a, far_b], axis=0), up


def scatter_z(keep, got, z):
    half = keep.shape[1] // 2

    def block(k):
        index = (z + k) % NZ
        return pick(keep, index).astype(F32) + pick(got, index).astype(F32)

    far = block(4).astype(BF16)
    fwd = shift(far[:half], "z", NZ, 1).astype(F32)
    bwd = shift(far[half:], "z", NZ, -1).astype(F32)
    mine = block(3)
    fwd = jnp.concatenate([mine[:half] + fwd, mine[half:]], axis=0)
    mine = block(-3)
    bwd = jnp.concatenate([mine[:half], mine[half:] + bwd], axis=0)
    for k in (2, 1):
        fwd = block(k) + shift(fwd.astype(BF16), "z", NZ, 1).astype(F32)
        bwd = block(-k) + shift(bwd.astype(BF16), "z", NZ, -1).astype(F32)
    fwd = shift(fwd.astype(BF16), "z", NZ, 1).astype(F32)
    bwd = shift(bwd.astype(BF16), "z", NZ, -1).astype(F32)
    return block(0) + fwd + bwd


def per_device(
    activations,
    cotangent,
    weight,
    queries,
    new_keys,
    new_values,
    key_cache,
    value_cache,
    cache_lengths,
):
    z, xh, core, y, xl = (lax.axis_index(a) for a in ("z", "xh", "c", "y", "xl"))
    cot_other = swap(cotangent, "xl")
    acts = gather_y(activations.T)

    blocks = weight.reshape(QB, NZ, QB).transpose(1, 0, 2)
    blocks = lax.all_to_all(blocks, "z", 0, 0, tiled=True)
    blocks = blocks.reshape(NY, 2, QB, QB)
    kept, sent = pick(blocks, xl, 1), pick(blocks, 1 - xl, 1)
    blocks = jnp.stack([kept, swap(sent, "xl")], axis=1)
    weight_here = jnp.stack([pick(blocks, (y - k) % NY) for k in range(NY)], axis=0)

    attended = attend(queries, new_keys, new_values, key_cache, value_cache, cache_lengths)
    local_rows, local_steps = queries.shape[0], queries.shape[1]
    count = local_rows * local_steps
    heads = attended.reshape(local_rows, 2, 2, local_steps, QB).transpose(1, 2, 0, 3, 4)
    heads = heads.reshape(2, 2, count, QB)
    heads = jnp.concatenate([pick(heads, core, 1), pick(heads, 1 - core, 1)], axis=-1)
    kept, sent = pick(heads, xh), pick(heads, 1 - xh)
    got = swap(sent, "xh")
    mixed = jnp.concatenate(
        [jnp.where(xh == 0, kept, got), jnp.where(xh == 0, got, kept)], axis=0
    )
    mixed = gather_z(mixed, z).reshape(NZ * 2 * count, 2 * QB)
    lefts = gather_y(mixed)

    chunks = [
        [(0, 0), (1, 0), (3, 0)],
        [(2, 0), (0, 1), (1, 1), (2, 1), (3, 1)],
    ]
    sums = {}
    for names in chunks:
        keep, send = grad_parts(core, names, acts, (cotangent, cot_other))
        part = scatter_z(keep, swap(send, "c"), z).reshape(len(names), 2, QB, QB)
        kept, sent = pick(part, xh, 1), pick(part, 1 - xh, 1)
        part = kept + swap(sent.astype(BF16), "xh").astype(F32)
        sums.update({name: part[n] for n, name in enumerate(names)})
    grad = jnp.stack(
        [jnp.stack([sums[k, h] for h in range(2)], axis=0) for k in range(NY)], axis=0
    )

    blocks = grad.astype(BF16)
    blocks = jnp.stack([pick(blocks, (y - k) % NY) for k in range(NY)], axis=0)
    kept, got = blocks[:, 0], swap(blocks[:, 1], "xl")
    first = jnp.where(xl == 0, kept, got)
    second = jnp.where(xl == 0, got, kept)
    blocks = jnp.stack([first, second], axis=1).reshape(NZ, QB, QB)
    blocks = lax.all_to_all(blocks, "z", 0, 0, tiled=True)
    grad_weight = blocks.transpose(1, 0, 2).reshape(QB, NZ * QB).astype(F32)

    updated = weight_here.astype(F32) - learn_rate * grad
    largest = jnp.max(jnp.abs(updated), axis=(2, 3))
    scales = ((largest + epsilon) / scale_limit).astype(BF16)
    quantized = (updated / scales.astype(F32)[:, :, None, None]).astype(BF16)
    quantized_other, scales_other = swap(quantized, "c"), swap(scales, "c")

    both = jnp.stack([scales, scales_other], axis=1).astype(F32).reshape(2 * NY, 2, 1)
    both = jnp.broadcast_to(both, (2 * NY, 2, QB)).reshape(2 * NY, 2 * QB)
    out = project(xl, lefts, quantized, quantized_other, both, count)
    out = out.reshape(NZ * 4, count, QB)
    out = lax.all_to_all(out, ("z", "xh", "xl"), 0, 0, tiled=True)
    out = out.reshape(NZ, 4, count, QB).astype(F32).sum(axis=1).astype(BF16)
    decoded = out.transpose(1, 0, 2).reshape(local_rows, local_steps, NZ * QB)
    return (grad_weight, decoded)


def solution(mesh):
    inner = Mesh(mesh.devices.reshape(8, 2, 2, 4, 2), ("z", "xh", "c", "y", "xl"))
    fsdp, tp = ("z", "xh", "c"), ("y", "xl")
    return jax.shard_map(
        per_device,
        mesh=inner,
        in_specs=(
            P(fsdp, tp),
            P(fsdp, tp),
            P(fsdp, tp),
            P(fsdp, None, tp, None, None),
            P(fsdp, None, tp, None),
            P(fsdp, None, tp, None),
            P(fsdp, tp, None, None),
            P(fsdp, tp, None, None),
            P(fsdp),
        ),
        out_specs=(P(fsdp, tp), P(fsdp, None, tp)),
        check_vma=False,
    )
```

```python
import functools

import jax
import jax.numpy as jnp
from jax import lax
from jax.experimental import pallas as pl
from jax.experimental.pallas import tpu as pltpu
from jax.sharding import Mesh, PartitionSpec as P

QB = 128
NZ = 8
NY = 4

learn_rate = 0.01
scale_limit = 448.0
epsilon = 1e-06

F32 = jnp.float32
BF16 = jnp.bfloat16
NT = (((1,), (1,)), ((), ()))


def shift(x, axis, size, step):
    return lax.ppermute(x, axis, [(i, (i + step) % size) for i in range(size)])


def swap(x, axis):
    return lax.ppermute(x, axis, [(0, 1), (1, 0)])


def after(x, *others):
    return lax.optimization_barrier((x, *others))[0]


def pick(x, index, axis=0):
    return lax.dynamic_index_in_dim(x, index, axis, keepdims=False)


def payload_kernel(steps, len_ref, q_ref, nk_ref, nv_ref, k_ref, v_ref, weight_ref, out_ref):
    rows, count, size = q_ref.shape
    breadth = weight_ref.shape[1]
    index = pl.program_id(0)

    @pl.when(index == 0)
    def _():
        for v in range(breadth // QB):
            out_ref[v * QB : (v + 1) * QB] = weight_ref[:, v * QB : (v + 1) * QB]

    factor = size ** (-0.5)
    first = index * rows
    places = lax.broadcasted_iota(jnp.int32, (count, k_ref.shape[1]), 1)
    step = lax.broadcasted_iota(jnp.int32, (count, nk_ref.shape[1]), 0) % steps
    later = lax.broadcasted_iota(jnp.int32, (count, nk_ref.shape[1]), 1) > step
    attended = []
    for r in range(rows):
        q = q_ref[r]
        old = lax.dot_general(q, k_ref[r], NT, preferred_element_type=F32) * factor
        new = lax.dot_general(q, nk_ref[r], NT, preferred_element_type=F32) * factor
        old = jnp.where(places < len_ref[first + r], old, -jnp.inf)
        new = jnp.where(later, -jnp.inf, new)
        top = jnp.maximum(
            jnp.max(old, axis=1, keepdims=True), jnp.max(new, axis=1, keepdims=True)
        )
        old, new = jnp.exp(old - top), jnp.exp(new - top)
        total = jnp.sum(old, axis=1, keepdims=True) + jnp.sum(new, axis=1, keepdims=True)
        old, new = (old / total).astype(BF16), (new / total).astype(BF16)
        mixed = jnp.dot(old, v_ref[r], preferred_element_type=F32)
        attended.append(mixed + jnp.dot(new, nv_ref[r], preferred_element_type=F32))
    for h in range(count // steps):
        block = [mixed[h * steps : (h + 1) * steps] for mixed in attended]
        block = jnp.concatenate(block, axis=0).astype(BF16)
        height = rows * steps
        start = breadth + h * height * pl.num_programs(0) + index * height
        out_ref[pl.ds(pl.multiple_of(start, height), height)] = block


def make_payload(queries, new_keys, new_values, key_cache, value_cache, cache_lengths, weight):
    rows, steps, _, heads, size = queries.shape
    cache = key_cache.shape[2]
    tile = 4
    q = queries[:, :, 0].transpose(0, 2, 1, 3).reshape(rows, heads * steps, size)
    pad = ((0, 0), (0, 16 - steps), (0, 0))
    nk, nv = jnp.pad(new_keys[:, :, 0], pad), jnp.pad(new_values[:, :, 0], pad)
    shape = (weight.shape[1] + heads * rows * steps, QB)

    def block(height):
        return pl.BlockSpec((tile, height, size), lambda i: (i, 0, 0))

    return pl.pallas_call(
        functools.partial(payload_kernel, steps),
        grid=(rows // tile,),
        out_shape=jax.ShapeDtypeStruct(shape, BF16),
        in_specs=[pl.BlockSpec(memory_space=pltpu.SMEM)]
        + [block(heads * steps), block(16), block(16), block(cache), block(cache)]
        + [pl.BlockSpec(weight.shape, lambda i: (0, 0))],
        out_specs=pl.BlockSpec(shape, lambda i: (0, 0)),
        cost_estimate=pl.CostEstimate(flops=2**34, bytes_accessed=2**22, transcendentals=0),
    )(cache_lengths, q, nk, nv, key_cache[:, 0], value_cache[:, 0], weight)


def grad_kernel(names, lefts, rights, core_ref, *refs):
    left_refs = dict(zip(lefts, refs))
    right_refs = dict(zip(rights, refs[len(lefts) :]))
    out_refs = refs[len(lefts) + len(rights) :]
    group = len(names) // (len(out_refs) // 2)
    own = core_ref[0] == 0
    for n, (left, right) in enumerate(names):
        part = jnp.dot(left_refs[left][...], right_refs[right][...], preferred_element_type=F32)
        part = part.astype(BF16)
        half = part.shape[0] // 2
        keep_ref, send_ref = out_refs[n // group * 2 : n // group * 2 + 2]
        for w in range(2):
            start = n % group * half + w * QB
            rows = slice(start, start + QB)
            for v in range(keep_ref.shape[0]):
                columns = slice(v * QB, (v + 1) * QB)
                low = part[2 * w * QB : (2 * w + 1) * QB, columns]
                high = part[(2 * w + 1) * QB : (2 * w + 2) * QB, columns]
                keep_ref[v, rows] = jnp.where(own, low, high)
                send_ref[v, rows] = jnp.where(own, high, low)


def grad_parts(core, names, left_arrays, right_arrays, group):
    lefts = sorted({left for left, _ in names})
    rights = sorted({right for _, right in names})
    height, depth = left_arrays[lefts[0]].shape
    breadth = right_arrays[rights[0]].shape[1]
    tile = 2 * QB
    rows = group * height // 2
    shape = jax.ShapeDtypeStruct((breadth // QB, rows, QB), BF16)
    out = pl.BlockSpec((tile // QB, rows, QB), lambda i: (i, 0, 0))
    copies = 2 * len(names) // group
    return pl.pallas_call(
        functools.partial(grad_kernel, names, lefts, rights),
        grid=(breadth // tile,),
        out_shape=(shape,) * copies,
        in_specs=[pl.BlockSpec(memory_space=pltpu.SMEM)]
        + [pl.BlockSpec((height, depth), lambda i: (0, 0))] * len(lefts)
        + [pl.BlockSpec((depth, tile), lambda i: (0, i))] * len(rights),
        out_specs=(out,) * copies,
        compiler_params=pltpu.CompilerParams(vmem_limit_bytes=40 * 2**20),
        cost_estimate=pl.CostEstimate(
            flops=2**20,
            bytes_accessed=2**10,
            transcendentals=0,
        ),
    )(core.reshape(1), *[left_arrays[n] for n in lefts], *[right_arrays[n] for n in rights])


def project_kernel(scale_ref, *refs):
    left_refs, (quant_ref, quant_other_ref), out_refs = refs[:NY], refs[NY : NY + 2], refs[NY + 2 :]
    tile, _, _, count, _ = left_refs[0].shape
    rows = tile * 2 * count
    total = jnp.zeros((rows, 2 * QB), F32)
    for k in range(NY):
        for j, quant in enumerate((quant_ref, quant_other_ref)):
            right = jnp.concatenate([quant[k, 0], quant[k, 1]], axis=1)
            product = jnp.dot(
                left_refs[k][:, :, j].reshape(rows, QB), right, preferred_element_type=F32
            )
            total = total + product * scale_ref[2 * k + j : 2 * k + j + 1, :]
    total = total.reshape(tile, 2, count, 2 * QB)
    for w in range(2):
        for v in range(2):
            out_refs[2 * w + v][...] = total[:, w, :, v * QB : (v + 1) * QB].astype(
                out_refs[2 * w + v].dtype
            )


def project(lefts, quantized, quantized_other, scales):
    tile = 2
    count = lefts[0].shape[3]
    whole = pl.BlockSpec(quantized.shape, lambda i: (0, 0, 0, 0))
    shape = (NZ, count, QB)
    return pl.pallas_call(
        project_kernel,
        grid=(NZ // tile,),
        out_shape=(jax.ShapeDtypeStruct(shape, F32),) + (jax.ShapeDtypeStruct(shape, BF16),) * 3,
        in_specs=[pl.BlockSpec(scales.shape, lambda i: (0, 0))]
        + [pl.BlockSpec((tile, 2, 2, count, QB), lambda i: (i, 0, 0, 0, 0))] * NY
        + [whole, whole],
        out_specs=(pl.BlockSpec((tile, count, QB), lambda i: (i, 0, 0)),) * 4,
        cost_estimate=pl.CostEstimate(
            flops=2 * NZ * 2 * count * 2 * QB * 8 * QB,
            bytes_accessed=4 * 2**20,
            transcendentals=0,
        ),
    )(scales, *lefts, quantized, quantized_other)


def gather_y(x):
    half = x.shape[0] // 2
    down = shift(x, "y", NY, 1)
    up = shift(x, "y", NY, -1)
    far_a = shift(down[:half], "y", NY, 1)
    far_b = shift(up[half:], "y", NY, -1)
    return x, down, jnp.concatenate([far_a, far_b], axis=0), up


def add_cores(outs):
    return [
        (keep.astype(F32) + swap(send, "c").astype(F32)).astype(BF16)
        for keep, send in zip(outs[::2], outs[1::2])
    ]


def z_block(pieces, index):
    return jnp.concatenate([pick(a, index) for a in pieces], axis=0).astype(F32)


def z_first(pieces, z):
    far = z_block(pieces, (z + 4) % NZ).astype(BF16)
    half = far.shape[0] // 2
    fwd = shift(far[:half], "z", NZ, 1).astype(F32)
    bwd = shift(far[half:], "z", NZ, -1).astype(F32)
    mine = z_block(pieces, (z + 3) % NZ)
    fwd = jnp.concatenate([mine[:half] + fwd, mine[half:]], axis=0)
    mine = z_block(pieces, (z - 3) % NZ)
    bwd = jnp.concatenate([mine[:half], mine[half:] + bwd], axis=0)
    return fwd.astype(BF16), bwd.astype(BF16)


def z_next(pieces, z, k, fwd, bwd):
    fwd = z_block(pieces, (z + k) % NZ) + shift(fwd, "z", NZ, 1).astype(F32)
    bwd = z_block(pieces, (z - k) % NZ) + shift(bwd, "z", NZ, -1).astype(F32)
    return fwd.astype(BF16), bwd.astype(BF16)


def z_last(pieces, z, fwd, bwd):
    fwd, bwd = shift(fwd, "z", NZ, 1), shift(bwd, "z", NZ, -1)
    return z_block(pieces, z) + fwd.astype(F32) + bwd.astype(F32)


def per_device(
    activations,
    cotangent,
    weight,
    queries,
    new_keys,
    new_values,
    key_cache,
    value_cache,
    cache_lengths,
):
    z, xh, core, y, xl = (lax.axis_index(a) for a in ("z", "xh", "c", "y", "xl"))
    cot_other = swap(cotangent, "xl")
    acts = gather_y(activations.T)

    local_rows, local_steps = queries.shape[0], queries.shape[1]
    count = local_rows * local_steps
    payload = make_payload(
        queries, new_keys, new_values, key_cache, value_cache, cache_lengths, weight
    )
    everyone = lax.all_gather(payload, "z", axis=0, tiled=False)

    early = [(0, 0), (1, 0)]
    late = [(2, 0), (3, 0)] + [(k, 1) for k in range(NY)]
    outs = grad_parts(core, early, acts, (after(cotangent, payload),), 1)
    pieces = add_cores(outs)
    cot_other = after(cot_other, *pieces)
    outs = grad_parts(core, late, acts, (cotangent, cot_other), 3)
    part = jnp.concatenate(add_cores(outs), axis=1)
    part = after(part, everyone)
    late_part = lax.psum_scatter(part, "z", scatter_dimension=0, tiled=False)

    blocks = lax.dynamic_slice_in_dim(everyone, z * QB, QB, axis=1).reshape(NY, 2, QB, QB)
    blocks = after(blocks, part)
    kept, sent = pick(blocks, xl, 1), pick(blocks, 1 - xl, 1)
    blocks = jnp.stack([kept, swap(sent, "xl")], axis=1)
    weight_here = jnp.stack([pick(blocks, (y - k) % NY) for k in range(NY)], axis=0)

    heads = everyone[:, NZ * QB :].reshape(NZ, 2, 2, count, QB)
    heads = jnp.stack([pick(heads, core, 2), pick(heads, 1 - core, 2)], axis=2)
    kept, sent = pick(heads, xh, 1), pick(heads, 1 - xh, 1)
    got = swap(after(sent, part), "xh")
    pieces = lax.optimization_barrier((*pieces, part))[:-1]
    ways = z_first(pieces, z)
    ways = z_next(pieces, z, 2, *ways)
    own = jnp.stack([kept, got], axis=1)
    down, up = shift(own, "y", NY, 1), shift(own, "y", NY, -1)
    ways = z_next(pieces, z, 1, *lax.optimization_barrier((*ways, own))[:2])
    far_a = shift(down[: NZ // 2], "y", NY, 1)
    far_b = shift(up[NZ // 2 :], "y", NY, -1)
    early_part = z_last(pieces, z, *lax.optimization_barrier((*ways, down, up))[:2])
    lefts = (own, down, jnp.concatenate([far_a, far_b], axis=0), up)

    sums = {}
    for names, part in ((early, early_part), (late, late_part)):
        part = part.reshape(len(names), 2, QB, QB)
        kept, sent = pick(part, xh, 1), pick(part, 1 - xh, 1)
        part = kept.astype(F32) + swap(sent.astype(BF16), "xh").astype(F32)
        sums.update({name: part[n] for n, name in enumerate(names)})
    grad = jnp.stack(
        [jnp.stack([sums[k, h] for h in range(2)], axis=0) for k in range(NY)], axis=0
    )

    updated = weight_here.astype(F32) - learn_rate * grad
    largest = jnp.max(jnp.abs(updated), axis=(2, 3))
    scales = ((largest + epsilon) / scale_limit).astype(BF16)
    quantized = (updated / scales.astype(F32)[:, :, None, None]).astype(BF16)
    quantized_other, scales_other = swap(quantized, "c"), swap(scales, "c")

    both = jnp.stack([scales, scales_other], axis=1).astype(F32).reshape(2 * NY, 2, 1)
    both = jnp.broadcast_to(both, (2 * NY, 2, QB)).reshape(2 * NY, 2 * QB)
    mine, to_lo, to_hi, to_both = project(lefts, quantized, quantized_other, both)
    out = (
        mine
        + swap(to_lo, "xl").astype(F32)
        + swap(to_hi, "xh").astype(F32)
        + lax.ppermute(to_both, ("xh", "xl"), [(i, 3 - i) for i in range(4)]).astype(F32)
    ).astype(BF16)

    blocks = grad.astype(BF16)
    blocks = jnp.stack([pick(blocks, (y - k) % NY) for k in range(NY)], axis=0)
    kept, got = blocks[:, 0], swap(blocks[:, 1], "xl")
    first = jnp.where(xl == 0, kept, got)
    second = jnp.where(xl == 0, got, kept)
    blocks = jnp.stack([first, second], axis=1).reshape(NZ, QB, QB)
    blocks = jnp.concatenate([out, blocks], axis=1)
    blocks = lax.all_to_all(blocks, "z", 0, 0, tiled=True).transpose(1, 0, 2)
    blocks = blocks.reshape(count + QB, NZ * QB)
    decoded = blocks[:count].reshape(local_rows, local_steps, NZ * QB)
    return (blocks[count:].astype(F32), decoded)


def solution(mesh):
    inner = Mesh(mesh.devices.reshape(8, 2, 2, 4, 2), ("z", "xh", "c", "y", "xl"))
    fsdp, tp = ("z", "xh", "c"), ("y", "xl")
    return jax.shard_map(
        per_device,
        mesh=inner,
        in_specs=(
            P(fsdp, tp),
            P(fsdp, tp),
            P(fsdp, tp),
            P(fsdp, None, tp, None, None),
            P(fsdp, None, tp, None),
            P(fsdp, None, tp, None),
            P(fsdp, tp, None, None),
            P(fsdp, tp, None, None),
            P(fsdp),
        ),
        out_specs=(P(fsdp, tp), P(fsdp, None, tp)),
        check_vma=False,
    )
```

```python
import functools

import jax
import jax.numpy as jnp
from jax import lax
from jax.experimental import pallas as pl
from jax.experimental.pallas import tpu as pltpu
from jax.sharding import Mesh, PartitionSpec as P

QB = 128
NZ = 8
NY = 4

learn_rate = 0.01
scale_limit = 448.0
epsilon = 1e-06

F32 = jnp.float32
BF16 = jnp.bfloat16
NT = (((1,), (1,)), ((), ()))


def shift(x, axis, size, step):
    return lax.ppermute(x, axis, [(i, (i + step) % size) for i in range(size)])


def swap(x, axis):
    return lax.ppermute(x, axis, [(0, 1), (1, 0)])


def after(x, *others):
    return lax.optimization_barrier((x, *others))[0]


def pick(x, index, axis=0):
    return lax.dynamic_index_in_dim(x, index, axis, keepdims=False)


def payload_kernel(steps, len_ref, q_ref, nk_ref, nv_ref, k_ref, v_ref, weight_ref, out_ref):
    rows, count, size = q_ref.shape
    breadth = weight_ref.shape[1]
    index = pl.program_id(0)

    @pl.when(index == 0)
    def _():
        for v in range(breadth // QB):
            out_ref[v * QB : (v + 1) * QB] = weight_ref[:, v * QB : (v + 1) * QB]

    factor = size ** (-0.5)
    first = index * rows
    places = lax.broadcasted_iota(jnp.int32, (count, k_ref.shape[1]), 1)
    step = lax.broadcasted_iota(jnp.int32, (count, nk_ref.shape[1]), 0) % steps
    later = lax.broadcasted_iota(jnp.int32, (count, nk_ref.shape[1]), 1) > step
    attended = []
    for r in range(rows):
        q = q_ref[r]
        old = lax.dot_general(q, k_ref[r], NT, preferred_element_type=F32) * factor
        new = lax.dot_general(q, nk_ref[r], NT, preferred_element_type=F32) * factor
        old = jnp.where(places < len_ref[first + r], old, -jnp.inf)
        new = jnp.where(later, -jnp.inf, new)
        top = jnp.maximum(
            jnp.max(old, axis=1, keepdims=True), jnp.max(new, axis=1, keepdims=True)
        )
        old, new = jnp.exp(old - top), jnp.exp(new - top)
        total = jnp.sum(old, axis=1, keepdims=True) + jnp.sum(new, axis=1, keepdims=True)
        old, new = (old / total).astype(BF16), (new / total).astype(BF16)
        mixed = jnp.dot(old, v_ref[r], preferred_element_type=F32)
        attended.append(mixed + jnp.dot(new, nv_ref[r], preferred_element_type=F32))
    for h in range(count // steps):
        block = [mixed[h * steps : (h + 1) * steps] for mixed in attended]
        block = jnp.concatenate(block, axis=0).astype(BF16)
        height = rows * steps
        start = breadth + h * height * pl.num_programs(0) + index * height
        out_ref[pl.ds(pl.multiple_of(start, height), height)] = block


def make_payload(queries, new_keys, new_values, key_cache, value_cache, cache_lengths, weight):
    rows, steps, _, heads, size = queries.shape
    cache = key_cache.shape[2]
    tile = 4
    q = queries[:, :, 0].transpose(0, 2, 1, 3).reshape(rows, heads * steps, size)
    pad = ((0, 0), (0, 16 - steps), (0, 0))
    nk, nv = jnp.pad(new_keys[:, :, 0], pad), jnp.pad(new_values[:, :, 0], pad)
    shape = (weight.shape[1] + heads * rows * steps, QB)

    def block(height):
        return pl.BlockSpec((tile, height, size), lambda i: (i, 0, 0))

    return pl.pallas_call(
        functools.partial(payload_kernel, steps),
        grid=(rows // tile,),
        out_shape=jax.ShapeDtypeStruct(shape, BF16),
        in_specs=[pl.BlockSpec(memory_space=pltpu.SMEM)]
        + [block(heads * steps), block(16), block(16), block(cache), block(cache)]
        + [pl.BlockSpec(weight.shape, lambda i: (0, 0))],
        out_specs=pl.BlockSpec(shape, lambda i: (0, 0)),
        cost_estimate=pl.CostEstimate(flops=2**34, bytes_accessed=2**22, transcendentals=0),
    )(cache_lengths, q, nk, nv, key_cache[:, 0], value_cache[:, 0], weight)


def grad_kernel(groups, lefts, rights, core_ref, *refs):
    left_refs = dict(zip(lefts, refs))
    right_refs = dict(zip(rights, refs[len(lefts) :]))
    out_refs = refs[len(lefts) + len(rights) :]
    own = core_ref[0] == 0
    for g, names in enumerate(groups):
        keep_ref, send_ref = out_refs[2 * g : 2 * g + 2]
        for n, (left, right) in enumerate(names):
            part = jnp.dot(
                left_refs[left][...], right_refs[right][...], preferred_element_type=F32
            ).astype(BF16)
            for w in range(2):
                rows = slice((2 * n + w) * QB, (2 * n + w + 1) * QB)
                for v in range(keep_ref.shape[0]):
                    columns = slice(v * QB, (v + 1) * QB)
                    low = part[2 * w * QB : (2 * w + 1) * QB, columns]
                    high = part[(2 * w + 1) * QB : (2 * w + 2) * QB, columns]
                    keep_ref[v, rows] = jnp.where(own, low, high)
                    send_ref[v, rows] = jnp.where(own, high, low)


def grad_parts(core, groups, left_arrays, right_arrays, moved):
    lefts = sorted({left for names in groups for left, _ in names})
    rights = sorted({right for names in groups for _, right in names})
    height, depth = left_arrays[lefts[0]].shape
    breadth = right_arrays[rights[0]].shape[1]
    tile = 2 * QB
    shapes, outs = [], []
    for names in groups:
        rows = len(names) * height // 2
        shapes += [jax.ShapeDtypeStruct((breadth // QB, rows, QB), BF16)] * 2
        outs += [pl.BlockSpec((tile // QB, rows, QB), lambda i: (i, 0, 0))] * 2
    return pl.pallas_call(
        functools.partial(grad_kernel, groups, lefts, rights),
        grid=(breadth // tile,),
        out_shape=tuple(shapes),
        in_specs=[pl.BlockSpec(memory_space=pltpu.SMEM)]
        + [pl.BlockSpec((height, depth), lambda i: (0, 0))] * len(lefts)
        + [pl.BlockSpec((depth, tile), lambda i: (0, i))] * len(rights),
        out_specs=tuple(outs),
        compiler_params=pltpu.CompilerParams(vmem_limit_bytes=40 * 2**20),
        cost_estimate=pl.CostEstimate(flops=2**20, bytes_accessed=moved, transcendentals=0),
    )(core.reshape(1), *[left_arrays[n] for n in lefts], *[right_arrays[n] for n in rights])


def project_kernel(*refs):
    left_refs, right_refs, out_refs = refs[: NY + 1], refs[NY + 1 : NY + 3], refs[NY + 3 :]
    tile, _, _, count, _ = left_refs[0].shape
    rows = tile * 2 * count
    lower = pl.program_id(0) < pl.num_programs(0) // 2
    total = 0.0
    for j, right in enumerate(right_refs):
        left = [left_ref[:, :, j].reshape(rows, QB) for left_ref in left_refs]
        left[2:4] = [jnp.where(lower, left[2], left[3])]
        left = jnp.concatenate(left, axis=1)
        total = total + jnp.dot(left, right[...], preferred_element_type=F32)
    total = total.reshape(tile, 2, count, 2 * QB)
    for w in range(2):
        for v in range(2):
            out_refs[2 * w + v][...] = total[:, w, :, v * QB : (v + 1) * QB].astype(
                out_refs[2 * w + v].dtype
            )


def project(lefts, right, right_other):
    tile = 4
    count = lefts[0].shape[3]
    whole = pl.BlockSpec(right.shape, lambda i: (0, 0))
    shape = (NZ, count, QB)
    steps = NZ // tile
    block = (tile, 2, 2, count, QB)
    whole_row = pl.BlockSpec(block, lambda i: (i, 0, 0, 0, 0))
    low_half = pl.BlockSpec(block, lambda i: (jnp.minimum(i, steps // 2 - 1), 0, 0, 0, 0))
    high_half = pl.BlockSpec(block, lambda i: (jnp.maximum(i - steps // 2, 0), 0, 0, 0, 0))
    return pl.pallas_call(
        project_kernel,
        grid=(NZ // tile,),
        out_shape=(jax.ShapeDtypeStruct(shape, F32),) + (jax.ShapeDtypeStruct(shape, BF16),) * 3,
        in_specs=[whole_row, whole_row, low_half, high_half, whole_row]
        + [whole, whole],
        out_specs=(pl.BlockSpec((tile, count, QB), lambda i: (i, 0, 0)),) * 4,
        cost_estimate=pl.CostEstimate(
            flops=2 * NZ * 2 * count * 2 * QB * 8 * QB,
            bytes_accessed=4 * 2**20,
            transcendentals=0,
        ),
    )(*lefts, right, right_other)


def gather_y(x):
    half = x.shape[0] // 2
    down = shift(x, "y", NY, 1)
    up = shift(x, "y", NY, -1)
    far_a = shift(down[:half], "y", NY, 1)
    far_b = shift(up[half:], "y", NY, -1)
    return x, down, jnp.concatenate([far_a, far_b], axis=0), up


def add_cores(outs):
    return [
        (keep.astype(F32) + swap(send, "c").astype(F32)).astype(BF16)
        for keep, send in zip(outs[::2], outs[1::2])
    ]


def z_block(pieces, index):
    return jnp.concatenate([pick(a, index) for a in pieces], axis=0).astype(F32)


def z_first(pieces, z):
    far = z_block(pieces, (z + 4) % NZ).astype(BF16)
    half = far.shape[0] // 2
    fwd = shift(far[:half], "z", NZ, 1).astype(F32)
    bwd = shift(far[half:], "z", NZ, -1).astype(F32)
    mine = z_block(pieces, (z + 3) % NZ)
    fwd = jnp.concatenate([mine[:half] + fwd, mine[half:]], axis=0)
    mine = z_block(pieces, (z - 3) % NZ)
    bwd = jnp.concatenate([mine[:half], mine[half:] + bwd], axis=0)
    return fwd.astype(BF16), bwd.astype(BF16)


def z_next(pieces, z, k, fwd, bwd):
    fwd = z_block(pieces, (z + k) % NZ) + shift(fwd, "z", NZ, 1).astype(F32)
    bwd = z_block(pieces, (z - k) % NZ) + shift(bwd, "z", NZ, -1).astype(F32)
    return fwd.astype(BF16), bwd.astype(BF16)


def z_last(pieces, z, fwd, bwd):
    fwd, bwd = shift(fwd, "z", NZ, 1), shift(bwd, "z", NZ, -1)
    return z_block(pieces, z) + fwd.astype(F32) + bwd.astype(F32)


def per_device(
    activations,
    cotangent,
    weight,
    queries,
    new_keys,
    new_values,
    key_cache,
    value_cache,
    cache_lengths,
):
    z, xh, core, y, xl = (lax.axis_index(a) for a in ("z", "xh", "c", "y", "xl"))
    cot_other = swap(cotangent, "xl")
    acts = gather_y(activations.T)

    local_rows, local_steps = queries.shape[0], queries.shape[1]
    count = local_rows * local_steps
    payload = make_payload(
        queries, new_keys, new_values, key_cache, value_cache, cache_lengths, weight
    )
    everyone = lax.all_gather(payload, "z", axis=0, tiled=False)

    early = [[(0, 0)], [(1, 0)]]
    late = [[(2, 0), (3, 0), (0, 1)], [(1, 1), (2, 1), (3, 1)]]
    outs = grad_parts(core, early, acts, (after(cotangent, payload),), 2**10)
    pieces = add_cores(outs)
    cot_other = after(cot_other, *pieces)
    outs = grad_parts(core, late, acts, (cotangent, cot_other), 2**10)
    part = jnp.concatenate(add_cores(outs), axis=1)
    part = after(part, everyone)
    early, late = [(0, 0), (1, 0)], late[0] + late[1]
    late_part = lax.psum_scatter(part, "z", scatter_dimension=0, tiled=False)

    blocks = lax.dynamic_slice_in_dim(everyone, z * QB, QB, axis=1).reshape(NY, 2, QB, QB)
    blocks = after(blocks, part)
    kept, sent = pick(blocks, xl, 1), pick(blocks, 1 - xl, 1)
    blocks = jnp.stack([kept, swap(sent, "xl")], axis=1)
    weight_here = jnp.stack([pick(blocks, (y - k) % NY) for k in range(NY)], axis=0)

    heads = everyone[:, NZ * QB :].reshape(NZ, 2, 2, count, QB)
    heads = jnp.stack([pick(heads, core, 2), pick(heads, 1 - core, 2)], axis=2)
    kept, sent = pick(heads, xh, 1), pick(heads, 1 - xh, 1)
    got = swap(after(sent, part), "xh")
    pieces = lax.optimization_barrier((*pieces, part))[:-1]
    ways = z_first(pieces, z)
    ways = z_next(pieces, z, 2, *ways)
    own = jnp.stack([kept, got], axis=1)
    down, up = shift(own, "y", NY, 1), shift(own, "y", NY, -1)
    ways = z_next(pieces, z, 1, *lax.optimization_barrier((*ways, own))[:2])
    far_a = shift(down[: NZ // 2], "y", NY, 1)
    far_b = shift(up[NZ // 2 :], "y", NY, -1)
    early_part = z_last(pieces, z, *lax.optimization_barrier((*ways, down, up))[:2])
    lefts = (own, down, far_a, far_b, up)

    sums = {}
    for names, part in ((early, early_part), (late, late_part)):
        part = part.reshape(len(names), 2, QB, QB)
        kept, sent = pick(part, xh, 1), pick(part, 1 - xh, 1)
        part = kept.astype(F32) + swap(sent.astype(BF16), "xh").astype(F32)
        sums.update({name: part[n] for n, name in enumerate(names)})
    grad = jnp.stack(
        [jnp.stack([sums[k, h] for h in range(2)], axis=0) for k in range(NY)], axis=0
    )

    updated = weight_here.astype(F32) - learn_rate * grad
    largest = jnp.max(jnp.abs(updated), axis=(2, 3))
    scales = ((largest + epsilon) / scale_limit).astype(BF16)
    quantized = (updated / scales.astype(F32)[:, :, None, None]).astype(BF16)
    right = (quantized.astype(F32) * scales.astype(F32)[:, :, None, None]).astype(BF16)
    right = right.transpose(0, 2, 1, 3).reshape(NY * QB, 2 * QB)

    mine, to_lo, to_hi, to_both = project(lefts, right, swap(right, "c"))
    out = (
        mine
        + swap(to_lo, "xl").astype(F32)
        + swap(to_hi, "xh").astype(F32)
        + lax.ppermute(to_both, ("xh", "xl"), [(i, 3 - i) for i in range(4)]).astype(F32)
    ).astype(BF16)

    blocks = after(grad.astype(BF16), mine)
    blocks = jnp.stack([pick(blocks, (y - k) % NY) for k in range(NY)], axis=0)
    kept, got = blocks[:, 0], swap(blocks[:, 1], "xl")
    first = jnp.where(xl == 0, kept, got)
    second = jnp.where(xl == 0, got, kept)
    blocks = jnp.stack([first, second], axis=1).reshape(NZ, QB, QB)
    blocks = jnp.concatenate([out, blocks], axis=1)
    blocks = lax.all_to_all(blocks, "z", 0, 0, tiled=True).transpose(1, 0, 2)
    blocks = blocks.reshape(count + QB, NZ * QB)
    decoded = blocks[:count].reshape(local_rows, local_steps, NZ * QB)
    return (blocks[count:].astype(F32), decoded)


def solution(mesh):
    inner = Mesh(mesh.devices.reshape(8, 2, 2, 4, 2), ("z", "xh", "c", "y", "xl"))
    fsdp, tp = ("z", "xh", "c"), ("y", "xl")
    return jax.shard_map(
        per_device,
        mesh=inner,
        in_specs=(
            P(fsdp, tp),
            P(fsdp, tp),
            P(fsdp, tp),
            P(fsdp, None, tp, None, None),
            P(fsdp, None, tp, None),
            P(fsdp, None, tp, None),
            P(fsdp, tp, None, None),
            P(fsdp, tp, None, None),
            P(fsdp),
        ),
        out_specs=(P(fsdp, tp), P(fsdp, None, tp)),
        check_vma=False,
    )
```

```python
import functools

import jax
import jax.numpy as jnp
from jax import lax
from jax.experimental import pallas as pl
from jax.experimental.pallas import tpu as pltpu
from jax.sharding import Mesh, PartitionSpec as P

QB = 128
NZ = 8
NY = 4

learn_rate = 0.01
scale_limit = 448.0
epsilon = 1e-06

F32 = jnp.float32
BF16 = jnp.bfloat16
NT = (((1,), (1,)), ((), ()))


def shift(x, axis, size, step):
    return lax.ppermute(x, axis, [(i, (i + step) % size) for i in range(size)])


def swap(x, axis):
    return lax.ppermute(x, axis, [(0, 1), (1, 0)])


def after(x, *others):
    return lax.optimization_barrier((x, *others))[0]


def pick(x, index, axis=0):
    return lax.dynamic_index_in_dim(x, index, axis, keepdims=False)


def payload_kernel(steps, len_ref, q_ref, nk_ref, nv_ref, k_ref, v_ref, weight_ref, out_ref):
    rows, count, size = q_ref.shape
    breadth = weight_ref.shape[1]
    index = pl.program_id(0)

    @pl.when(index == 0)
    def _():
        for v in range(breadth // QB):
            out_ref[v * QB : (v + 1) * QB] = weight_ref[:, v * QB : (v + 1) * QB]

    factor = size ** (-0.5)
    first = index * rows
    places = lax.broadcasted_iota(jnp.int32, (count, k_ref.shape[1]), 1)
    step = lax.broadcasted_iota(jnp.int32, (count, nk_ref.shape[1]), 0) % steps
    later = lax.broadcasted_iota(jnp.int32, (count, nk_ref.shape[1]), 1) > step
    attended = []
    for r in range(rows):
        q = q_ref[r]
        old = lax.dot_general(q, k_ref[r], NT, preferred_element_type=F32) * factor
        new = lax.dot_general(q, nk_ref[r], NT, preferred_element_type=F32) * factor
        old = jnp.where(places < len_ref[first + r], old, -jnp.inf)
        new = jnp.where(later, -jnp.inf, new)
        top = jnp.maximum(
            jnp.max(old, axis=1, keepdims=True), jnp.max(new, axis=1, keepdims=True)
        )
        old, new = jnp.exp(old - top), jnp.exp(new - top)
        total = jnp.sum(old, axis=1, keepdims=True) + jnp.sum(new, axis=1, keepdims=True)
        old, new = (old / total).astype(BF16), (new / total).astype(BF16)
        mixed = jnp.dot(old, v_ref[r], preferred_element_type=F32)
        attended.append(mixed + jnp.dot(new, nv_ref[r], preferred_element_type=F32))
    for h in range(count // steps):
        block = [mixed[h * steps : (h + 1) * steps] for mixed in attended]
        block = jnp.concatenate(block, axis=0).astype(BF16)
        height = rows * steps
        start = breadth + h * height * pl.num_programs(0) + index * height
        out_ref[pl.ds(pl.multiple_of(start, height), height)] = block


def make_payload(queries, new_keys, new_values, key_cache, value_cache, cache_lengths, weight):
    rows, steps, _, heads, size = queries.shape
    cache = key_cache.shape[2]
    tile = 4
    q = queries[:, :, 0].transpose(0, 2, 1, 3).reshape(rows, heads * steps, size)
    pad = ((0, 0), (0, 16 - steps), (0, 0))
    nk, nv = jnp.pad(new_keys[:, :, 0], pad), jnp.pad(new_values[:, :, 0], pad)
    shape = (weight.shape[1] + heads * rows * steps, QB)

    def block(height):
        return pl.BlockSpec((tile, height, size), lambda i: (i, 0, 0))

    return pl.pallas_call(
        functools.partial(payload_kernel, steps),
        grid=(rows // tile,),
        out_shape=jax.ShapeDtypeStruct(shape, BF16),
        in_specs=[pl.BlockSpec(memory_space=pltpu.SMEM)]
        + [block(heads * steps), block(16), block(16), block(cache), block(cache)]
        + [pl.BlockSpec(weight.shape, lambda i: (0, 0))],
        out_specs=pl.BlockSpec(shape, lambda i: (0, 0)),
        cost_estimate=pl.CostEstimate(flops=2**34, bytes_accessed=2**22, transcendentals=0),
    )(cache_lengths, q, nk, nv, key_cache[:, 0], value_cache[:, 0], weight)


def grad_kernel(groups, lefts, rights, core_ref, *refs):
    left_refs = dict(zip(lefts, refs))
    right_refs = dict(zip(rights, refs[len(lefts) :]))
    out_refs = refs[len(lefts) + len(rights) :]
    own = core_ref[0] == 0
    for g, names in enumerate(groups):
        keep_ref, send_ref = out_refs[2 * g : 2 * g + 2]
        for n, (left, right) in enumerate(names):
            part = jnp.dot(
                left_refs[left][...], right_refs[right][...], preferred_element_type=F32
            ).astype(BF16)
            for w in range(2):
                rows = slice((2 * n + w) * QB, (2 * n + w + 1) * QB)
                for v in range(keep_ref.shape[0]):
                    columns = slice(v * QB, (v + 1) * QB)
                    low = part[2 * w * QB : (2 * w + 1) * QB, columns]
                    high = part[(2 * w + 1) * QB : (2 * w + 2) * QB, columns]
                    keep_ref[v, rows] = jnp.where(own, low, high)
                    send_ref[v, rows] = jnp.where(own, high, low)


def grad_parts(core, groups, left_arrays, right_arrays, moved):
    lefts = sorted({left for names in groups for left, _ in names})
    rights = sorted({right for names in groups for _, right in names})
    height, depth = left_arrays[lefts[0]].shape
    breadth = right_arrays[rights[0]].shape[1]
    tile = 2 * QB
    shapes, outs = [], []
    for names in groups:
        rows = len(names) * height // 2
        shapes += [jax.ShapeDtypeStruct((breadth // QB, rows, QB), BF16)] * 2
        outs += [pl.BlockSpec((tile // QB, rows, QB), lambda i: (i, 0, 0))] * 2
    return pl.pallas_call(
        functools.partial(grad_kernel, groups, lefts, rights),
        grid=(breadth // tile,),
        out_shape=tuple(shapes),
        in_specs=[pl.BlockSpec(memory_space=pltpu.SMEM)]
        + [pl.BlockSpec((height, depth), lambda i: (0, 0))] * len(lefts)
        + [pl.BlockSpec((depth, tile), lambda i: (0, i))] * len(rights),
        out_specs=tuple(outs),
        compiler_params=pltpu.CompilerParams(vmem_limit_bytes=40 * 2**20),
        cost_estimate=pl.CostEstimate(flops=2**20, bytes_accessed=moved, transcendentals=0),
    )(core.reshape(1), *[left_arrays[n] for n in lefts], *[right_arrays[n] for n in rights])


def project_kernel(*refs):
    left_refs, right_refs, out_refs = refs[: NY + 1], refs[NY + 1 : NY + 3], refs[NY + 3 :]
    tile, _, _, count, _ = left_refs[0].shape
    rows = tile * 2 * count
    lower = pl.program_id(0) < pl.num_programs(0) // 2
    total = 0.0
    for j, right in enumerate(right_refs):
        left = [left_ref[:, :, j].reshape(rows, QB) for left_ref in left_refs]
        left[2:4] = [jnp.where(lower, left[2], left[3])]
        left = jnp.concatenate(left, axis=1)
        total = total + jnp.dot(left, right[...], preferred_element_type=F32)
    total = total.reshape(tile, 2, count, 2 * QB)
    for w in range(2):
        for v in range(2):
            out_refs[2 * w + v][...] = total[:, w, :, v * QB : (v + 1) * QB].astype(
                out_refs[2 * w + v].dtype
            )


def project(lefts, right, right_other):
    tile = 4
    count = lefts[0].shape[3]
    whole = pl.BlockSpec(right.shape, lambda i: (0, 0))
    shape = (NZ, count, QB)
    steps = NZ // tile
    block = (tile, 2, 2, count, QB)
    whole_row = pl.BlockSpec(block, lambda i: (i, 0, 0, 0, 0))
    low_half = pl.BlockSpec(block, lambda i: (jnp.minimum(i, steps // 2 - 1), 0, 0, 0, 0))
    high_half = pl.BlockSpec(block, lambda i: (jnp.maximum(i - steps // 2, 0), 0, 0, 0, 0))
    return pl.pallas_call(
        project_kernel,
        grid=(NZ // tile,),
        out_shape=(jax.ShapeDtypeStruct(shape, F32),) + (jax.ShapeDtypeStruct(shape, BF16),) * 3,
        in_specs=[whole_row, whole_row, low_half, high_half, whole_row]
        + [whole, whole],
        out_specs=(pl.BlockSpec((tile, count, QB), lambda i: (i, 0, 0)),) * 4,
        cost_estimate=pl.CostEstimate(
            flops=2 * NZ * 2 * count * 2 * QB * 8 * QB,
            bytes_accessed=4 * 2**20,
            transcendentals=0,
        ),
    )(*lefts, right, right_other)


def gather_y(x):
    half = x.shape[0] // 2
    down = shift(x, "y", NY, 1)
    up = shift(x, "y", NY, -1)
    far_a = shift(down[:half], "y", NY, 1)
    far_b = shift(up[half:], "y", NY, -1)
    return x, down, jnp.concatenate([far_a, far_b], axis=0), up


def add_cores(outs):
    return [
        (keep.astype(F32) + swap(send, "c").astype(F32)).astype(BF16)
        for keep, send in zip(outs[::2], outs[1::2])
    ]


def z_block(pieces, index):
    return jnp.concatenate([pick(a, index) for a in pieces], axis=0).astype(F32)


def z_first(pieces, z):
    far = z_block(pieces, (z + 4) % NZ).astype(BF16)
    half = far.shape[0] // 2
    fwd = shift(far[:half], "z", NZ, 1).astype(F32)
    bwd = shift(far[half:], "z", NZ, -1).astype(F32)
    mine = z_block(pieces, (z + 3) % NZ)
    fwd = jnp.concatenate([mine[:half] + fwd, mine[half:]], axis=0)
    mine = z_block(pieces, (z - 3) % NZ)
    bwd = jnp.concatenate([mine[:half], mine[half:] + bwd], axis=0)
    return fwd.astype(BF16), bwd.astype(BF16)


def z_next(pieces, z, k, fwd, bwd):
    fwd = z_block(pieces, (z + k) % NZ) + shift(fwd, "z", NZ, 1).astype(F32)
    bwd = z_block(pieces, (z - k) % NZ) + shift(bwd, "z", NZ, -1).astype(F32)
    return fwd.astype(BF16), bwd.astype(BF16)


def z_last(pieces, z, fwd, bwd):
    fwd, bwd = shift(fwd, "z", NZ, 1), shift(bwd, "z", NZ, -1)
    return z_block(pieces, z) + fwd.astype(F32) + bwd.astype(F32)


def per_device(
    activations,
    cotangent,
    weight,
    queries,
    new_keys,
    new_values,
    key_cache,
    value_cache,
    cache_lengths,
):
    z, xh, core, y, xl = (lax.axis_index(a) for a in ("z", "xh", "c", "y", "xl"))
    cot_other = swap(cotangent, "xl")
    acts = gather_y(activations.T)

    local_rows, local_steps = queries.shape[0], queries.shape[1]
    count = local_rows * local_steps
    payload = make_payload(
        queries, new_keys, new_values, key_cache, value_cache, cache_lengths, weight
    )
    everyone = lax.all_gather(payload, "z", axis=0, tiled=False)

    early = [[(0, 0)], [(1, 0)]]
    late = [[(2, 0), (3, 0), (0, 1)], [(1, 1), (2, 1), (3, 1)]]
    outs = grad_parts(core, early, acts, (after(cotangent, payload),), 2**10)
    pieces = add_cores(outs)
    cot_other = after(cot_other, *pieces)
    outs = grad_parts(core, late, acts, (cotangent, cot_other), 2**10)
    part = jnp.concatenate(add_cores(outs), axis=1)
    part = after(part, everyone)
    early, late = [(0, 0), (1, 0)], late[0] + late[1]
    late_part = lax.psum_scatter(part, "z", scatter_dimension=0, tiled=False)

    blocks = lax.dynamic_slice_in_dim(everyone, z * QB, QB, axis=1).reshape(NY, 2, QB, QB)
    blocks = after(blocks, part)
    kept, sent = pick(blocks, xl, 1), pick(blocks, 1 - xl, 1)
    blocks = jnp.stack([kept, swap(sent, "xl")], axis=1)
    weight_here = jnp.stack([pick(blocks, (y - k) % NY) for k in range(NY)], axis=0)

    heads = everyone[:, NZ * QB :].reshape(NZ, 2, 2, count, QB)
    heads = jnp.stack([pick(heads, core, 2), pick(heads, 1 - core, 2)], axis=2)
    kept, sent = pick(heads, xh, 1), pick(heads, 1 - xh, 1)
    pieces = lax.optimization_barrier((*pieces, part))[:-1]
    ways = z_first(pieces, z)
    got = swap(after(sent, *ways), "xh")
    ways = z_next(pieces, z, 2, *ways)
    own = jnp.stack([kept, got], axis=1)
    down, up = shift(own, "y", NY, 1), shift(own, "y", NY, -1)
    ways = z_next(pieces, z, 1, *lax.optimization_barrier((*ways, own))[:2])
    far_a = shift(down[: NZ // 2], "y", NY, 1)
    far_b = shift(up[NZ // 2 :], "y", NY, -1)
    early_part = z_last(pieces, z, *lax.optimization_barrier((*ways, down, up))[:2])
    lefts = (own, down, far_a, far_b, up)

    sums = {}
    for names, part in ((early, early_part), (late, late_part)):
        part = part.reshape(len(names), 2, QB, QB)
        kept, sent = pick(part, xh, 1), pick(part, 1 - xh, 1)
        part = kept.astype(F32) + swap(sent.astype(BF16), "xh").astype(F32)
        sums.update({name: part[n] for n, name in enumerate(names)})
    grad = jnp.stack(
        [jnp.stack([sums[k, h] for h in range(2)], axis=0) for k in range(NY)], axis=0
    )

    updated = weight_here.astype(F32) - learn_rate * grad
    largest = jnp.max(jnp.abs(updated), axis=(2, 3))
    scales = ((largest + epsilon) / scale_limit).astype(BF16)
    quantized = (updated / scales.astype(F32)[:, :, None, None]).astype(BF16)
    right = (quantized.astype(F32) * scales.astype(F32)[:, :, None, None]).astype(BF16)
    right = right.transpose(0, 2, 1, 3).reshape(NY * QB, 2 * QB)

    mine, to_lo, to_hi, to_both = project(lefts, right, swap(right, "c"))
    out = (
        mine
        + swap(to_lo, "xl").astype(F32)
        + swap(to_hi, "xh").astype(F32)
        + lax.ppermute(to_both, ("xh", "xl"), [(i, 3 - i) for i in range(4)]).astype(F32)
    ).astype(BF16)

    blocks = after(grad.astype(BF16), mine)
    blocks = jnp.stack([pick(blocks, (y - k) % NY) for k in range(NY)], axis=0)
    kept, got = blocks[:, 0], swap(blocks[:, 1], "xl")
    first = jnp.where(xl == 0, kept, got)
    second = jnp.where(xl == 0, got, kept)
    blocks = jnp.stack([first, second], axis=1).reshape(NZ, QB, QB)
    blocks = jnp.concatenate([out, blocks], axis=1)
    blocks = lax.all_to_all(blocks, "z", 0, 0, tiled=True).transpose(1, 0, 2)
    blocks = blocks.reshape(count + QB, NZ * QB)
    decoded = blocks[:count].reshape(local_rows, local_steps, NZ * QB)
    return (blocks[count:].astype(F32), decoded)


def solution(mesh):
    inner = Mesh(mesh.devices.reshape(8, 2, 2, 4, 2), ("z", "xh", "c", "y", "xl"))
    fsdp, tp = ("z", "xh", "c"), ("y", "xl")
    return jax.shard_map(
        per_device,
        mesh=inner,
        in_specs=(
            P(fsdp, tp),
            P(fsdp, tp),
            P(fsdp, tp),
            P(fsdp, None, tp, None, None),
            P(fsdp, None, tp, None),
            P(fsdp, None, tp, None),
            P(fsdp, tp, None, None),
            P(fsdp, tp, None, None),
            P(fsdp),
        ),
        out_specs=(P(fsdp, tp), P(fsdp, None, tp)),
        check_vma=False,
    )
```

```python
import functools

import jax
import jax.numpy as jnp
from jax import lax
from jax.experimental import pallas as pl
from jax.experimental.pallas import tpu as pltpu
from jax.sharding import Mesh, PartitionSpec as P

QB = 128
NZ = 8
NY = 4

learn_rate = 0.01
scale_limit = 448.0
epsilon = 1e-06

F32 = jnp.float32
BF16 = jnp.bfloat16
NT = (((1,), (1,)), ((), ()))


def shift(x, axis, size, step):
    return lax.ppermute(x, axis, [(i, (i + step) % size) for i in range(size)])


def swap(x, axis):
    return lax.ppermute(x, axis, [(0, 1), (1, 0)])


def after(x, *others):
    return lax.optimization_barrier((x, *others))[0]


def pick(x, index, axis=0):
    return lax.dynamic_index_in_dim(x, index, axis, keepdims=False)


def payload_kernel(steps, len_ref, q_ref, nk_ref, nv_ref, k_ref, v_ref, weight_ref, out_ref):
    rows, count, size = q_ref.shape
    breadth = weight_ref.shape[1]
    index = pl.program_id(0)

    @pl.when(index == 0)
    def _():
        for v in range(breadth // QB):
            out_ref[v * QB : (v + 1) * QB] = weight_ref[:, v * QB : (v + 1) * QB]

    factor = size ** (-0.5)
    first = index * rows
    places = lax.broadcasted_iota(jnp.int32, (count, k_ref.shape[1]), 1)
    step = lax.broadcasted_iota(jnp.int32, (count, nk_ref.shape[1]), 0) % steps
    later = lax.broadcasted_iota(jnp.int32, (count, nk_ref.shape[1]), 1) > step
    attended = []
    for r in range(rows):
        q = q_ref[r]
        old = lax.dot_general(q, k_ref[r], NT, preferred_element_type=F32) * factor
        new = lax.dot_general(q, nk_ref[r], NT, preferred_element_type=F32) * factor
        old = jnp.where(places < len_ref[first + r], old, -jnp.inf)
        new = jnp.where(later, -jnp.inf, new)
        top = jnp.maximum(
            jnp.max(old, axis=1, keepdims=True), jnp.max(new, axis=1, keepdims=True)
        )
        old, new = jnp.exp(old - top), jnp.exp(new - top)
        total = jnp.sum(old, axis=1, keepdims=True) + jnp.sum(new, axis=1, keepdims=True)
        old, new = (old / total).astype(BF16), (new / total).astype(BF16)
        mixed = jnp.dot(old, v_ref[r], preferred_element_type=F32)
        attended.append(mixed + jnp.dot(new, nv_ref[r], preferred_element_type=F32))
    for h in range(count // steps):
        block = [mixed[h * steps : (h + 1) * steps] for mixed in attended]
        block = jnp.concatenate(block, axis=0).astype(BF16)
        height = rows * steps
        start = breadth + h * height * pl.num_programs(0) + index * height
        out_ref[pl.ds(pl.multiple_of(start, height), height)] = block


def make_payload(queries, new_keys, new_values, key_cache, value_cache, cache_lengths, weight):
    rows, steps, _, heads, size = queries.shape
    cache = key_cache.shape[2]
    tile = 4
    q = queries[:, :, 0].transpose(0, 2, 1, 3).reshape(rows, heads * steps, size)
    pad = ((0, 0), (0, 16 - steps), (0, 0))
    nk, nv = jnp.pad(new_keys[:, :, 0], pad), jnp.pad(new_values[:, :, 0], pad)
    shape = (weight.shape[1] + heads * rows * steps, QB)

    def block(height):
        return pl.BlockSpec((tile, height, size), lambda i: (i, 0, 0))

    return pl.pallas_call(
        functools.partial(payload_kernel, steps),
        grid=(rows // tile,),
        out_shape=jax.ShapeDtypeStruct(shape, BF16),
        in_specs=[pl.BlockSpec(memory_space=pltpu.SMEM)]
        + [block(heads * steps), block(16), block(16), block(cache), block(cache)]
        + [pl.BlockSpec(weight.shape, lambda i: (0, 0))],
        out_specs=pl.BlockSpec(shape, lambda i: (0, 0)),
        cost_estimate=pl.CostEstimate(flops=2**34, bytes_accessed=2**22, transcendentals=0),
    )(cache_lengths, q, nk, nv, key_cache[:, 0], value_cache[:, 0], weight)


def grad_kernel(groups, lefts, rights, core_ref, *refs):
    left_refs = dict(zip(lefts, refs))
    right_refs = dict(zip(rights, refs[len(lefts) :]))
    out_refs = refs[len(lefts) + len(rights) :]
    own = core_ref[0] == 0
    for g, names in enumerate(groups):
        keep_ref, send_ref = out_refs[2 * g : 2 * g + 2]
        for n, (left, right) in enumerate(names):
            part = jnp.dot(
                left_refs[left][...], right_refs[right][...], preferred_element_type=F32
            ).astype(BF16)
            for w in range(2):
                rows = slice((2 * n + w) * QB, (2 * n + w + 1) * QB)
                for v in range(keep_ref.shape[0]):
                    columns = slice(v * QB, (v + 1) * QB)
                    low = part[2 * w * QB : (2 * w + 1) * QB, columns]
                    high = part[(2 * w + 1) * QB : (2 * w + 2) * QB, columns]
                    keep_ref[v, rows] = jnp.where(own, low, high)
                    send_ref[v, rows] = jnp.where(own, high, low)


def grad_parts(core, groups, left_arrays, right_arrays, moved):
    lefts = sorted({left for names in groups for left, _ in names})
    rights = sorted({right for names in groups for _, right in names})
    height, depth = left_arrays[lefts[0]].shape
    breadth = right_arrays[rights[0]].shape[1]
    tile = 2 * QB
    shapes, outs = [], []
    for names in groups:
        rows = len(names) * height // 2
        shapes += [jax.ShapeDtypeStruct((breadth // QB, rows, QB), BF16)] * 2
        outs += [pl.BlockSpec((tile // QB, rows, QB), lambda i: (i, 0, 0))] * 2
    return pl.pallas_call(
        functools.partial(grad_kernel, groups, lefts, rights),
        grid=(breadth // tile,),
        out_shape=tuple(shapes),
        in_specs=[pl.BlockSpec(memory_space=pltpu.SMEM)]
        + [pl.BlockSpec((height, depth), lambda i: (0, 0))] * len(lefts)
        + [pl.BlockSpec((depth, tile), lambda i: (0, i))] * len(rights),
        out_specs=tuple(outs),
        compiler_params=pltpu.CompilerParams(vmem_limit_bytes=40 * 2**20),
        cost_estimate=pl.CostEstimate(flops=2**20, bytes_accessed=moved, transcendentals=0),
    )(core.reshape(1), *[left_arrays[n] for n in lefts], *[right_arrays[n] for n in rights])


def project_kernel(*refs):
    left_refs, right_refs, out_refs = refs[: NY + 1], refs[NY + 1 : NY + 3], refs[NY + 3 :]
    tile, _, _, count, _ = left_refs[0].shape
    rows = tile * 2 * count
    lower = pl.program_id(0) < pl.num_programs(0) // 2
    total = 0.0
    for j, right in enumerate(right_refs):
        left = [left_ref[:, :, j].reshape(rows, QB) for left_ref in left_refs]
        left[2:4] = [jnp.where(lower, left[2], left[3])]
        left = jnp.concatenate(left, axis=1)
        total = total + jnp.dot(left, right[...], preferred_element_type=F32)
    total = total.reshape(tile, 2, count, 2 * QB)
    for w in range(2):
        for v in range(2):
            out_refs[2 * w + v][...] = total[:, w, :, v * QB : (v + 1) * QB].astype(
                out_refs[2 * w + v].dtype
            )


def project(lefts, right, right_other):
    tile = 4
    count = lefts[0].shape[3]
    whole = pl.BlockSpec(right.shape, lambda i: (0, 0))
    shape = (NZ, count, QB)
    steps = NZ // tile
    block = (tile, 2, 2, count, QB)
    whole_row = pl.BlockSpec(block, lambda i: (i, 0, 0, 0, 0))
    low_half = pl.BlockSpec(block, lambda i: (jnp.minimum(i, steps // 2 - 1), 0, 0, 0, 0))
    high_half = pl.BlockSpec(block, lambda i: (jnp.maximum(i - steps // 2, 0), 0, 0, 0, 0))
    return pl.pallas_call(
        project_kernel,
        grid=(NZ // tile,),
        out_shape=(jax.ShapeDtypeStruct(shape, F32),) + (jax.ShapeDtypeStruct(shape, BF16),) * 3,
        in_specs=[whole_row, whole_row, low_half, high_half, whole_row]
        + [whole, whole],
        out_specs=(pl.BlockSpec((tile, count, QB), lambda i: (i, 0, 0)),) * 4,
        cost_estimate=pl.CostEstimate(
            flops=2 * NZ * 2 * count * 2 * QB * 8 * QB,
            bytes_accessed=4 * 2**20,
            transcendentals=0,
        ),
    )(*lefts, right, right_other)


def gather_y(x):
    half = x.shape[0] // 2
    down = shift(x, "y", NY, 1)
    up = shift(x, "y", NY, -1)
    far_a = shift(down[:half], "y", NY, 1)
    far_b = shift(up[half:], "y", NY, -1)
    return x, down, jnp.concatenate([far_a, far_b], axis=0), up


def add_cores(outs):
    return [
        (keep.astype(F32) + swap(send, "c").astype(F32)).astype(BF16)
        for keep, send in zip(outs[::2], outs[1::2])
    ]


def z_block(pieces, index):
    return jnp.concatenate([pick(a, index) for a in pieces], axis=0).astype(F32)


def z_first(pieces, z):
    far = z_block(pieces, (z + 4) % NZ).astype(BF16)
    half = far.shape[0] // 2
    fwd = shift(far[:half], "z", NZ, 1).astype(F32)
    bwd = shift(far[half:], "z", NZ, -1).astype(F32)
    mine = z_block(pieces, (z + 3) % NZ)
    fwd = jnp.concatenate([mine[:half] + fwd, mine[half:]], axis=0)
    mine = z_block(pieces, (z - 3) % NZ)
    bwd = jnp.concatenate([mine[:half], mine[half:] + bwd], axis=0)
    return fwd.astype(BF16), bwd.astype(BF16)


def z_next(pieces, z, k, fwd, bwd):
    fwd = z_block(pieces, (z + k) % NZ) + shift(fwd, "z", NZ, 1).astype(F32)
    bwd = z_block(pieces, (z - k) % NZ) + shift(bwd, "z", NZ, -1).astype(F32)
    return fwd.astype(BF16), bwd.astype(BF16)


def z_last(pieces, z, fwd, bwd):
    fwd, bwd = shift(fwd, "z", NZ, 1), shift(bwd, "z", NZ, -1)
    return z_block(pieces, z) + fwd.astype(F32) + bwd.astype(F32)


def per_device(
    activations,
    cotangent,
    weight,
    queries,
    new_keys,
    new_values,
    key_cache,
    value_cache,
    cache_lengths,
):
    z, xh, core, y, xl = (lax.axis_index(a) for a in ("z", "xh", "c", "y", "xl"))
    cot_other = swap(cotangent, "xl")
    acts = gather_y(activations.T)

    local_rows, local_steps = queries.shape[0], queries.shape[1]
    count = local_rows * local_steps
    payload = make_payload(
        queries, new_keys, new_values, key_cache, value_cache, cache_lengths, weight
    )
    everyone = lax.all_gather(payload, "z", axis=0, tiled=False)

    early = [[(0, 0)], [(1, 0)]]
    late = [[(2, 0), (3, 0), (0, 1)], [(1, 1), (2, 1), (3, 1)]]
    outs = grad_parts(core, early, acts, (after(cotangent, payload),), 2**10)
    pieces = add_cores(outs)
    cot_other = after(cot_other, *pieces)
    outs = grad_parts(core, late, acts, (cotangent, cot_other), 2**10)
    part = jnp.concatenate(add_cores(outs), axis=1)
    part = after(part, everyone)
    early, late = [(0, 0), (1, 0)], late[0] + late[1]
    late_part = lax.psum_scatter(part, "z", scatter_dimension=0, tiled=False)

    heads = everyone[:, NZ * QB :].reshape(NZ, 2, 2, count, QB)
    heads = jnp.stack([pick(heads, core, 2), pick(heads, 1 - core, 2)], axis=2)
    kept, sent = pick(heads, xh, 1), pick(heads, 1 - xh, 1)
    pieces = lax.optimization_barrier((*pieces, part))[:-1]
    ways = z_first(pieces, z)
    got = swap(after(sent, *ways), "xh")
    first_hop = ways
    ways = z_next(pieces, z, 2, *ways)
    own = jnp.stack([kept, got], axis=1)
    down, up = shift(own, "y", NY, 1), shift(own, "y", NY, -1)
    ways = z_next(pieces, z, 1, *lax.optimization_barrier((*ways, own))[:2])
    far_a = shift(down[: NZ // 2], "y", NY, 1)
    far_b = shift(up[NZ // 2 :], "y", NY, -1)
    early_part = z_last(pieces, z, *lax.optimization_barrier((*ways, down, up))[:2])
    lefts = (own, down, far_a, far_b, up)

    blocks = lax.dynamic_slice_in_dim(everyone, z * QB, QB, axis=1).reshape(NY, 2, QB, QB)
    blocks = after(blocks, *first_hop)
    kept, sent = pick(blocks, xl, 1), pick(blocks, 1 - xl, 1)
    blocks = jnp.stack([kept, swap(sent, "xl")], axis=1)
    weight_here = jnp.stack([pick(blocks, (y - k) % NY) for k in range(NY)], axis=0)

    sums = {}
    for names, part in ((early, early_part), (late, late_part)):
        part = part.reshape(len(names), 2, QB, QB)
        kept, sent = pick(part, xh, 1), pick(part, 1 - xh, 1)
        part = kept.astype(F32) + swap(sent.astype(BF16), "xh").astype(F32)
        sums.update({name: part[n] for n, name in enumerate(names)})
    grad = jnp.stack(
        [jnp.stack([sums[k, h] for h in range(2)], axis=0) for k in range(NY)], axis=0
    )

    updated = weight_here.astype(F32) - learn_rate * grad
    largest = jnp.max(jnp.abs(updated), axis=(2, 3))
    scales = ((largest + epsilon) / scale_limit).astype(BF16)
    quantized = (updated / scales.astype(F32)[:, :, None, None]).astype(BF16)
    right = (quantized.astype(F32) * scales.astype(F32)[:, :, None, None]).astype(BF16)
    right = right.transpose(0, 2, 1, 3).reshape(NY * QB, 2 * QB)

    mine, to_lo, to_hi, to_both = project(lefts, right, swap(right, "c"))
    out = (
        mine
        + swap(to_lo, "xl").astype(F32)
        + swap(to_hi, "xh").astype(F32)
        + lax.ppermute(to_both, ("xh", "xl"), [(i, 3 - i) for i in range(4)]).astype(F32)
    ).astype(BF16)

    blocks = after(grad.astype(BF16), mine)
    blocks = jnp.stack([pick(blocks, (y - k) % NY) for k in range(NY)], axis=0)
    kept, got = blocks[:, 0], swap(blocks[:, 1], "xl")
    first = jnp.where(xl == 0, kept, got)
    second = jnp.where(xl == 0, got, kept)
    blocks = jnp.stack([first, second], axis=1).reshape(NZ, QB, QB)
    blocks = jnp.concatenate([out, blocks], axis=1)
    blocks = lax.all_to_all(blocks, "z", 0, 0, tiled=True).transpose(1, 0, 2)
    blocks = blocks.reshape(count + QB, NZ * QB)
    decoded = blocks[:count].reshape(local_rows, local_steps, NZ * QB)
    return (blocks[count:].astype(F32), decoded)


def solution(mesh):
    inner = Mesh(mesh.devices.reshape(8, 2, 2, 4, 2), ("z", "xh", "c", "y", "xl"))
    fsdp, tp = ("z", "xh", "c"), ("y", "xl")
    return jax.shard_map(
        per_device,
        mesh=inner,
        in_specs=(
            P(fsdp, tp),
            P(fsdp, tp),
            P(fsdp, tp),
            P(fsdp, None, tp, None, None),
            P(fsdp, None, tp, None),
            P(fsdp, None, tp, None),
            P(fsdp, tp, None, None),
            P(fsdp, tp, None, None),
            P(fsdp),
        ),
        out_specs=(P(fsdp, tp), P(fsdp, None, tp)),
        check_vma=False,
    )
```
